32 devices in a mesh: groups: 2 (over x), frame: 16 (over z, y, core).
Axes of the slice: x: 2, y: 2, z: 4, core: 2. Of those that a mesh axis runs over, the one named last changes fastest.
Arguments:
- query_rows: bfloat16 [8192, 2560], P(('groups', 'frame')), parts along dimension 0, may hold values from -60 to 60
- key_rows: bfloat16 [8192, 2560], P(('groups', 'frame')), parts along dimension 0, may hold values from -4 to 4
- value_rows: bfloat16 [8192, 2560], P(('groups', 'frame')), parts along dimension 0, may hold values from -6 to 6
- tile_mask: int32 [128, 27], P(('groups', 'frame')), parts along dimension 0, may hold values from 0 to 1, as said below
- head_weight: bfloat16 [2560, 64], replicated, may hold values from -0.125 to 0.125
- latent: float32 [8192, 64], P(('groups', 'frame')), parts along dimension 0, may hold values from -6 to 6
- step_index: int32 [2], P('groups'), parts along dimension 0, may hold values from 0 to 24
Outputs:
- guided: float32 [8192, 64], P(('groups', 'frame')), parts along dimension 0
- clean: float32 [8192, 64], P(('groups', 'frame')), parts along dimension 0
- latent_next: float32 [8192, 64], P(('groups', 'frame')), parts along dimension 0
The draws below stay inside these ranges and needn't reach their ends.
There are 2 independent parts, one for each index of `groups`. The reference program is written for one: setup_inputs(seed, part) draws one part's arguments, and reference() takes and returns one part's arrays. A program takes and returns all parts, laid end to end along the dimension named above; an argument that names none is the same for every part. Nothing has to cross between parts.
Inputs may be any that keep to these rules, and one draw needn't show every extreme that they name: `tile_mask`: entries are 0 or 1; entry 13 (the query tile itself) is always 1.
All inputs are finite; a program needn't handle non-finite values.
Results may differ from the reference program's by a relative error of at most 0.0041.
Values may be sent and summed in bfloat16 or wider, within the bound.
A program may use at most 128 MiB of HBM per device.

```python
import math
import jax
import jax.numpy as jnp
from jax import lax

HEADS = 20
HD = 128
CH = 64
SH = 4
SW = 8
SAMPLE_STEPS = 50
TILE_TOK = 64
NFT = 1
TOKENS = 2048
QT = 64
INNER = 2560


def joint_draw(key):
    base = jax.random.fold_in(key, 7)
    first, second = jax.random.split(base, 2)
    total_rows = 2 * TOKENS
    width = HEADS * HD
    keys_done = jnp.clip(jax.random.normal(first, (total_rows, width), jnp.float32), -4.0, 4.0)
    query_done = jnp.clip(2.0 * jax.random.normal(second, (total_rows, width), jnp.float32), -8.0, 8.0)
    return (query_done, keys_done)


def draw_query_rows(key, part):
    return joint_draw(key)[0].astype(jnp.bfloat16)


def draw_key_rows(key, part):
    return joint_draw(key)[1].astype(jnp.bfloat16)


def draw_tile_mask(key, part):
    base = jax.random.fold_in(key, 11)
    first, second, third = jax.random.split(base, 3)
    tile_count = 4
    slab_count = QT // tile_count
    slab_number = jnp.arange(slab_count, dtype=jnp.int32)[:, None, None]
    full_slab = slab_number % 4 == 0
    density = jax.random.randint(first, (slab_count, 1, 1), 15, 91)
    density = jnp.where(full_slab, 101, density)
    sides = jax.random.randint(second, (slab_count, 1, 3), 0, 4)
    plane_on = (sides != 0) | (jnp.arange(3, dtype=jnp.int32)[None, None, :] == 1) | full_slab
    draws = jax.random.randint(third, (slab_count, tile_count, 27), 0, 100)
    window_code = jnp.arange(27, dtype=jnp.int32)
    plane = window_code // 9
    plane_entry = jnp.take_along_axis(plane_on, jnp.broadcast_to(plane[None, None, :], (slab_count, 1, 27)), axis=2)
    entries = (draws < density) & plane_entry
    entries = entries | (window_code == 13)[None, None, :]
    return entries.astype(jnp.int32).reshape(QT, 27)


def levels(own_key, dims, pieces, low, largest):
    def one(position, blocks):
        steps = jax.random.uniform(jax.random.fold_in(jax.random.fold_in(own_key, 6), position), (blocks,), jnp.float32, low / len(pieces), largest / len(pieces))
        return jnp.repeat(jnp.exp(steps), dims[position] // blocks).reshape((-1,) + (1,) * (len(dims) - position - 1))

    level = one(*pieces[0])
    for cut in pieces[1:]:
        level = level * one(*cut)
    return level


def centred(key, dims, spread, reach, cuts=(), kind=jnp.bfloat16):
    values = spread * jax.random.normal(key, dims, jnp.float32)
    if cuts:
        values = values * levels(key, dims, cuts, -0.22, 0.18)
    return jnp.clip(values, -reach, reach).astype(kind)


def setup_inputs(seed: int = 0, part: int = 0) -> dict:
    keys = jax.random.split(jax.random.key(seed), 8)
    own_keys = jax.random.split(jax.random.fold_in(keys[7], part), 8)
    query_rows = draw_query_rows(jax.random.fold_in(jax.random.fold_in(keys[7], part), 71), part)
    key_rows = draw_key_rows(jax.random.fold_in(jax.random.fold_in(keys[7], part), 71), part)
    value_rows = centred(own_keys[2], (2 * TOKENS, INNER), 1.0, 6.0, ((0, 16),))
    tile_mask = draw_tile_mask(jax.random.fold_in(jax.random.fold_in(keys[7], part), 71), part)
    head_weight = centred(keys[4], (INNER, CH), INNER ** -0.5, 0.125)
    latent = centred(own_keys[5], (2 * TOKENS, CH), 1.0, 6.0, ((0, 16),), jnp.float32)
    step_index = jax.random.randint(own_keys[6], (1,), 0, SAMPLE_STEPS // 2).astype(jnp.int32)
    return dict(query_rows=query_rows, key_rows=key_rows, value_rows=value_rows, tile_mask=tile_mask, head_weight=head_weight, latent=latent, step_index=step_index)


GUIDANCE = 5.0
FLOW_SHIFT = 5.0

def flow_sigma(moment):
    remain = 1.0 - moment / SAMPLE_STEPS
    return FLOW_SHIFT * remain / (1.0 + (FLOW_SHIFT - 1.0) * remain)

def to_grid(rows):
    width = rows.shape[1]
    grid = rows.reshape(2, NFT, SH // 2, SW // 2, 2, 2, TILE_TOK, width)
    grid = grid.transpose(0, 1, 2, 4, 3, 5, 6, 7)
    return grid.reshape(2, NFT, SH, SW, TILE_TOK, width)

def attend_tile(query_tile, key_window, value_window, key_usable):
    query_float = query_tile.astype(jnp.float32).reshape(-1, HEADS, HD)
    key_float = key_window.astype(jnp.float32).reshape(-1, HEADS, HD)
    value_float = value_window.astype(jnp.float32).reshape(-1, HEADS, HD)
    scores = jnp.einsum('qhd,khd->hqk', query_float, key_float) / math.sqrt(HD)
    scores = jnp.where(key_usable[None, None, :], scores, -1e+30)
    row_max = lax.optimization_barrier(jnp.max(scores, axis=2, keepdims=True))
    shifted = jnp.where(key_usable[None, None, :], jnp.exp(scores - row_max), 0.0)
    weights = (shifted / lax.optimization_barrier(jnp.sum(shifted, axis=2, keepdims=True))).astype(jnp.bfloat16)
    result_rows = jnp.einsum('hqk,khd->qhd', weights.astype(jnp.float32), value_float)
    return result_rows.reshape(-1, HEADS * HD).astype(jnp.bfloat16)

def reference(query_rows, key_rows, value_rows, tile_mask, head_weight, latent, step_index):
    padding = ((0, 0), (1, 1), (1, 1), (1, 1), (0, 0), (0, 0))
    query_grid = to_grid(query_rows)
    key_pad = jnp.pad(to_grid(key_rows), padding)
    value_pad = jnp.pad(to_grid(value_rows), padding)
    mask_grid = tile_mask.reshape(2, NFT, SH // 2, SW // 2, 2, 2, 27).transpose(0, 1, 2, 4, 3, 5, 6).reshape(2, NFT, SH, SW, 27)
    offsets = jnp.arange(27, dtype=jnp.int32)
    frame_step = offsets // 9 - 1
    row_step = offsets // 3 % 3 - 1
    col_step = offsets % 3 - 1
    zero = jnp.zeros((), jnp.int32)

    def one_tile(tile_number):
        branch = tile_number // (NFT * SH * SW)
        frame_tile = tile_number // (SH * SW) % NFT
        tile_row = tile_number // SW % SH
        tile_col = tile_number % SW
        starts = (branch, frame_tile, tile_row, tile_col, zero, zero)
        query_tile = lax.dynamic_slice(query_grid, starts, (1, 1, 1, 1, TILE_TOK, INNER)).reshape(TILE_TOK, INNER)
        key_window = lax.dynamic_slice(key_pad, starts, (1, 3, 3, 3, TILE_TOK, INNER)).reshape(27 * TILE_TOK, INNER)
        value_window = lax.dynamic_slice(value_pad, starts, (1, 3, 3, 3, TILE_TOK, INNER)).reshape(27 * TILE_TOK, INNER)
        mask_row = lax.dynamic_slice(mask_grid, (branch, frame_tile, tile_row, tile_col, zero), (1, 1, 1, 1, 27)).reshape(27)
        frame_there = frame_tile + frame_step
        row_there = tile_row + row_step
        col_there = tile_col + col_step
        usable = (frame_there >= 0) & (frame_there < NFT) & (row_there >= 0) & (row_there < SH)
        usable = usable & (col_there >= 0) & (col_there < SW) & (mask_row > 0)
        key_usable = jnp.repeat(usable, TILE_TOK)
        attention = attend_tile(query_tile, key_window, value_window, key_usable)
        return jnp.dot(attention, head_weight, preferred_element_type=jnp.float32)
    velocity_grid = lax.map(one_tile, jnp.arange(2 * NFT * SH * SW, dtype=jnp.int32))
    velocity = velocity_grid.reshape(2, NFT, SH // 2, 2, SW // 2, 2, TILE_TOK, CH)
    velocity = velocity.transpose(0, 1, 2, 4, 3, 5, 6, 7).reshape(2, TOKENS, CH)
    blended = velocity[1] + GUIDANCE * (velocity[0] - velocity[1])
    guided = jnp.concatenate([blended, blended], axis=0)
    moment = step_index[0].astype(jnp.float32)
    sigma_now = flow_sigma(moment)
    step_size = flow_sigma(moment + 1.0) - sigma_now
    clean = latent - sigma_now * guided
    latent_next = latent + step_size * guided
    return (guided, clean, latent_next)
```

```python
import functools
import math

import jax
import jax.numpy as jnp
from jax import lax
from jax.experimental import pallas as pl
from jax.experimental.pallas import tpu as pltpu
from jax.sharding import PartitionSpec as P

HEADS = 20
HD = 128
SH = 4
SW = 8
SAMPLE_STEPS = 50
GUIDANCE = 5.0
FLOW_SHIFT = 5.0

NT = (((1,), (1,)), ((), ()))
F32 = jnp.float32
BF16 = jnp.bfloat16

GR = SH // 2 + 1
GC = SW // 2 + 1
SLOTS = GR * GC


def flow_sigma(moment):
    remain = 1.0 - moment / SAMPLE_STEPS
    return FLOW_SHIFT * remain / (1.0 + (FLOW_SHIFT - 1.0) * remain)


def kernel(
    planes, tile_frames, tok, ch,
    q_hbm, k_hbm, v_hbm, mask_ref, wt_ref,
    out_ref,
    kwin, vwin, qwin, mwin, vloc, vsrc, wbuf, vel, vsib, vpart,
    k_sem, v_sem, q_sem, m_sem, x_sem,
    ks_send, vs_send, qs_send, m_send, x_send,
):
    half = q_hbm.shape[1] // 2
    pairs = half // (2 * HD)
    f = lax.axis_index("frame")
    c = f % 2
    pcol = f // 2 % 2
    prow = f // 4 % 2
    ft = f // 8 % tile_frames
    branch = f // (8 * tile_frames)
    sibling = f + 1 - 2 * c
    partner = f + 8 * tile_frames * (1 - 2 * branch)
    dvert = 4 - 8 * prow
    dhoriz = 2 - 4 * pcol
    base_even = f - c
    edge_u = 1 - prow
    edge_v = 1 - pcol
    own_base = 2 * (pcol * c + (1 - pcol) * (1 - c))
    sib_base = 2 - own_base
    steps = [0] + ([-1, 1] if planes == 3 else [])

    def plane_of(df):
        return df + 1 if planes == 3 else 0

    def exists(df):
        return jnp.logical_and(ft + df >= 0, ft + df < tile_frames)

    def guard(df, extra=None):
        conds = []
        if df != 0:
            conds.append(exists(df))
        if extra is not None:
            conds.append(extra)
        if not conds:
            return lambda fn: fn()
        return pl.when(functools.reduce(jnp.logical_and, conds))

    v_copy = pltpu.make_async_copy(v_hbm, vloc, x_sem.at[2])
    v_copy.start()

    def rel(u, i):
        ur = prow * u + (1 - prow) * (1 - u)
        v = pcol * i + (1 - pcol) * (1 - i)
        return ur, v

    local = []
    for u in range(2):
        for i in range(2):
            ur, v = rel(u, i)
            row = pl.multiple_of((u * 2 + v) * tok, tok)
            wr = own_base + i
            slot = (1 + ur) * GC + 1 + wr
            cols = pl.ds(pl.multiple_of(c * half, half), half)
            pltpu.make_async_copy(
                k_hbm.at[pl.ds(row, tok), cols],
                kwin.at[plane_of(0), slot], k_sem.at[plane_of(0), slot]).start()
            pltpu.make_async_copy(
                q_hbm.at[pl.ds(row, tok), cols],
                qwin.at[wr * 2 + ur], q_sem.at[wr * 2 + ur]).start()

    barrier = pltpu.get_barrier_semaphore()
    block = f - f % 8
    greeted = 0
    for df in steps:
        for other in range(8):
            target = block + 8 * df + other
            if df == 0:
                @pl.when(target != f)
                def _(target=target):
                    pl.semaphore_signal(barrier, inc=1, device_id={"frame": target},
                                        device_id_type=pl.DeviceIdType.MESH)
            else:
                @pl.when(exists(df))
                def _(target=target):
                    pl.semaphore_signal(barrier, inc=1, device_id={"frame": target},
                                        device_id_type=pl.DeviceIdType.MESH)
        if df == 0:
            greeted = 7
        else:
            greeted = greeted + 8 * exists(df).astype(jnp.int32)
    pl.semaphore_signal(barrier, inc=1, device_id={"frame": partner},
                        device_id_type=pl.DeviceIdType.MESH)
    pl.semaphore_wait(barrier, greeted + 1)

    sends = []
    number = 0
    edge_core = c == 1 - pcol
    for df in steps:
        there = plane_of(-df)
        for core in range(2):
            target = base_even + 8 * df + core + dvert
            for i in range(2):
                v = pcol * i + (1 - pcol) * (1 - i)
                sends.append((df, None, target, core, edge_u * 2 + v,
                              0 * GC + 1 + own_base + i, there))
        for core in range(2):
            target = base_even + 8 * df + core + dvert + dhoriz
            sends.append((df, edge_core, target, core, edge_u * 2 + edge_v, 0, there))
        for core in range(2):
            target = base_even + 8 * df + core + dhoriz
            for u in range(2):
                ur = prow * u + (1 - prow) * (1 - u)
                sends.append((df, edge_core, target, core, u * 2 + edge_v,
                              (1 + ur) * GC, there))
        for u in range(2):
            for i in range(2):
                ur, v = rel(u, i)
                slot = (1 + ur) * GC + 1 + own_base + i
                if df == 0:
                    sends.append((df, None, sibling, None, u * 2 + v, slot, there))
                else:
                    for core in range(2):
                        sends.append((df, None, base_even + 8 * df + core, core,
                                      u * 2 + v, slot, there))

    def k_copy(n):
        df, cond, target, core, tile, slot, there = sends[n]
        core = 1 - c if core is None else core
        return pltpu.make_async_remote_copy(
            src_ref=k_hbm.at[pl.ds(pl.multiple_of(tile * tok, tok), tok),
                             pl.ds(pl.multiple_of(core * half, half), half)],
            dst_ref=kwin.at[there, slot],
            send_sem=ks_send.at[n], recv_sem=k_sem.at[there, slot],
            device_id={"frame": target}, device_id_type=pl.DeviceIdType.MESH)

    def v_copy_out(n):
        df, cond, target, core, tile, slot, there = sends[n]
        core = 1 - c if core is None else core
        return pltpu.make_async_remote_copy(
            src_ref=vsrc.at[tile, core],
            dst_ref=vwin.at[there, slot],
            send_sem=vs_send.at[n], recv_sem=v_sem.at[there, slot],
            device_id={"frame": target}, device_id_type=pl.DeviceIdType.MESH)

    def each_send(make, act):
        for n, (df, cond, *_) in enumerate(sends):
            guard(df, cond)(lambda n=n: act(make(n)))

    each_send(k_copy, lambda copy: copy.start())

    def q_copy(u, i):
        ur, v = rel(u, i)
        place = (own_base + i) * 2 + ur
        return pltpu.make_async_remote_copy(
            src_ref=q_hbm.at[pl.ds(pl.multiple_of((u * 2 + v) * tok, tok), tok),
                             pl.ds(pl.multiple_of((1 - c) * half, half), half)],
            dst_ref=qwin.at[place],
            send_sem=qs_send.at[u * 2 + i], recv_sem=q_sem.at[place],
            device_id={"frame": sibling}, device_id_type=pl.DeviceIdType.MESH)

    for u in range(2):
        for i in range(2):
            q_copy(u, i).start()

    lane = lax.broadcasted_iota(jnp.int32, (1, 2 * tok), 1)
    for i in range(2):
        v = pcol * i + (1 - pcol) * (1 - i)
        for df in steps:
            for rr in range(GR):
                for dj in range(3):
                    col = pcol * dj + (1 - pcol) * (2 - dj)
                    row0 = prow * rr + (1 - prow) * (2 - rr)
                    first = mask_ref[edge_u * 2 + v, 9 * (df + 1) + 3 * row0 + col]
                    if rr > 0:
                        row1 = prow * (rr - 1) + (1 - prow) * (3 - rr)
                        second = mask_ref[prow * 2 + v, 9 * (df + 1) + 3 * row1 + col]
                    else:
                        second = 0
                    value = jnp.where(lane < tok, first, second)
                    if df != 0:
                        value = value * exists(df).astype(jnp.int32)
                    mwin[own_base + i, pl.ds((plane_of(df) * GR + rr) * 3 + dj, 1), :] = (
                        jnp.where(value > 0, 3e38, -1e30).astype(F32))
    m_copy = pltpu.make_async_remote_copy(
        src_ref=mwin.at[pl.ds(own_base, 2)], dst_ref=mwin.at[pl.ds(own_base, 2)],
        send_sem=m_send.at[0], recv_sem=m_sem.at[0],
        device_id={"frame": sibling}, device_id_type=pl.DeviceIdType.MESH)
    m_copy.start()

    v_copy.wait()

    def project(j, _):
        parts = []
        for e in range(2):
            cols = pl.ds(pl.multiple_of((2 * j + e) * HD, HD), HD)
            parts.append(lax.dot_general(wt_ref[:, cols], vloc[:, cols], NT,
                                         preferred_element_type=F32))
        side = j // pairs
        rows = pl.ds(pl.multiple_of((j % pairs) * ch, ch), ch)
        for t in range(4):
            both = jnp.concatenate(
                [part[:, t * tok:(t + 1) * tok] for part in parts], axis=1).astype(BF16)
            vsrc[t, side, rows, :] = both
        return 0

    lax.fori_loop(0, 2 * pairs, project, 0)
    each_send(v_copy_out, lambda copy: copy.start())
    for u in range(2):
        for i in range(2):
            ur, v = rel(u, i)
            slot = (1 + ur) * GC + 1 + own_base + i
            vwin[plane_of(0), slot] = vsrc[u * 2 + v, c]
    for df in steps[1:]:
        @pl.when(jnp.logical_not(exists(df)))
        def _(df=df):
            kwin[plane_of(df)] = jnp.zeros(kwin.shape[1:], kwin.dtype)
            vwin[plane_of(df)] = jnp.zeros(vwin.shape[1:], vwin.dtype)

    for place in range(8):
        pltpu.make_async_copy(qwin.at[place], qwin.at[place], q_sem.at[place]).wait()
    m_back = pltpu.make_async_remote_copy(
        src_ref=mwin.at[pl.ds(sib_base, 2)], dst_ref=mwin.at[pl.ds(sib_base, 2)],
        send_sem=m_send.at[0], recv_sem=m_sem.at[0],
        device_id={"frame": sibling}, device_id_type=pl.DeviceIdType.MESH)
    m_back.wait_recv()
    for df in steps:
        def arrive(df=df):
            p = plane_of(df)
            for slot in range(SLOTS):
                pltpu.make_async_copy(kwin.at[p, slot], kwin.at[p, slot],
                                      k_sem.at[p, slot]).wait()
        guard(df)(arrive)

    scale = math.log2(math.e) / math.sqrt(HD)

    def weigh(hp, _):
        for wr in range(4):
            ncol = min(3, GC - wr)
            for e in range(2):
                cols = pl.ds(pl.multiple_of((2 * hp + e) * HD, HD), HD)
                query = qwin[2 * wr:2 * wr + 2, :, cols].reshape(2 * tok, HD)
                blocks = []
                top = None
                for p in range(planes):
                    for rr in range(GR):
                        first = rr * GC + wr
                        keys = kwin[p, first:first + ncol, :, cols].reshape(ncol * tok, HD)
                        s = lax.dot_general(keys, query, NT, preferred_element_type=F32)
                        for dj in range(ncol):
                            line = (p * GR + rr) * 3 + dj
                            part = jnp.minimum(s[dj * tok:(dj + 1) * tok] * scale,
                                               mwin[wr, line:line + 1, :])
                            blocks.append(part)
                            here = jnp.max(part.reshape(tok // 8, 8, 2 * tok), axis=0)
                            top = here if top is None else jnp.maximum(top, here)
                top = jnp.max(top, axis=0, keepdims=True)
                total = None
                grown = []
                for part in blocks:
                    g = jnp.exp2(part - top)
                    grown.append(g)
                    here = jnp.sum(g.reshape(tok // 8, 8, 2 * tok), axis=0)
                    total = here if total is None else total + here
                inverse = 1.0 / jnp.sum(total, axis=0, keepdims=True)
                for n, g in enumerate(grown):
                    start = n * 2 * tok + e * tok
                    wbuf[hp, wr, start:start + tok, :] = (g * inverse).astype(BF16)
        return 0

    lax.fori_loop(0, pairs, weigh, 0)

    own_half_slots = own_base + 1
    for df in steps:
        def arrive(df=df):
            p = plane_of(df)
            for slot in range(SLOTS):
                copy = pltpu.make_async_copy(vwin.at[p, slot], vwin.at[p, slot], v_sem.at[p, slot])
                rr, cc = slot // GC, slot % GC
                if df == 0 and rr > 0 and cc > 0:
                    side = (cc - 1) // 2
                    pl.when(own_base != 2 * side)(lambda copy=copy: copy.wait())
                else:
                    copy.wait()
        guard(df)(arrive)

    def gather(hp, acc):
        rows = pl.ds(pl.multiple_of(hp * ch, ch), ch)
        result = []
        for wr in range(4):
            ncol = min(3, GC - wr)
            total = acc[wr]
            n = 0
            for p in range(planes):
                for rr in range(GR):
                    for dj in range(ncol):
                        slot = rr * GC + wr + dj
                        total = total + jnp.dot(
                            vwin[p, slot, rows, :],
                            wbuf[hp, wr, n * 2 * tok:(n + 1) * 2 * tok, :],
                            preferred_element_type=F32)
                        n += 1
            result.append(total)
        return tuple(result)

    acc = lax.fori_loop(0, pairs, gather,
                        tuple(jnp.zeros((ch, 2 * tok), F32) for _ in range(4)))
    for wr in range(4):
        vel[wr] = acc[wr]

    s_copy = pltpu.make_async_remote_copy(
        src_ref=vel.at[pl.ds(sib_base, 2)], dst_ref=vsib.at[0],
        send_sem=x_send.at[0], recv_sem=x_sem.at[0],
        device_id={"frame": sibling}, device_id_type=pl.DeviceIdType.MESH)
    s_copy.start()
    s_copy.wait_recv()
    mine = vel[pl.ds(own_base, 2)] + vsib[0]
    vsib[1] = mine
    p_copy = pltpu.make_async_remote_copy(
        src_ref=vsib.at[1], dst_ref=vpart,
        send_sem=x_send.at[1], recv_sem=x_sem.at[1],
        device_id={"frame": partner}, device_id_type=pl.DeviceIdType.MESH)
    p_copy.start()
    p_copy.wait_recv()
    other = vpart[...]
    is_cond = branch == 0
    cond = jnp.where(is_cond, mine, other)
    uncond = jnp.where(is_cond, other, mine)
    guided = uncond + GUIDANCE * (cond - uncond)
    for i in range(2):
        v = pcol * i + (1 - pcol) * (1 - i)
        turned = guided[i].T
        out_ref[pl.ds(pl.multiple_of((edge_u * 2 + v) * tok, tok), tok), :] = turned[:tok]
        out_ref[pl.ds(pl.multiple_of((prow * 2 + v) * tok, tok), tok), :] = turned[tok:]

    each_send(k_copy, lambda copy: copy.wait_send())
    each_send(v_copy_out, lambda copy: copy.wait_send())
    for u in range(2):
        for i in range(2):
            q_copy(u, i).wait_send()
    m_copy.wait_send()
    s_copy.wait_send()
    p_copy.wait_send()


def per_device(query_rows, key_rows, value_rows, tile_mask, head_weight, latent, step_index):
    frame_count = lax.axis_size("frame")
    tile_frames = frame_count // (2 * (SH // 2) * (SW // 2))
    planes = 3 if tile_frames > 1 else 1
    rows, width = query_rows.shape
    tok = rows // 4
    ch = head_weight.shape[1]
    half = width // 2
    pairs = half // (2 * HD)
    n_sends = 14 + (planes - 1) * 18
    lines = -(-planes * GR * 3 // 8) * 8
    dma = pltpu.SemaphoreType.DMA
    hbm = pl.BlockSpec(memory_space=pl.ANY)
    guided = pl.pallas_call(
        functools.partial(kernel, planes, tile_frames, tok, ch),
        out_shape=jax.ShapeDtypeStruct((rows, ch), F32),
        in_specs=[hbm, hbm, hbm, pl.BlockSpec(memory_space=pltpu.SMEM),
                  pl.BlockSpec(memory_space=pltpu.VMEM)],
        out_specs=pl.BlockSpec(memory_space=pltpu.VMEM),
        scratch_shapes=[
            pltpu.VMEM((planes, SLOTS, tok, half), BF16),
            pltpu.VMEM((planes, SLOTS, pairs * ch, 2 * tok), BF16),
            pltpu.VMEM((8, tok, half), BF16),
            pltpu.VMEM((4, lines, 2 * tok), F32),
            pltpu.VMEM((rows, width), BF16),
            pltpu.VMEM((4, 2, pairs * ch, 2 * tok), BF16),
            pltpu.VMEM((pairs, 4, planes * GR * 3 * 2 * tok, 2 * tok), BF16),
            pltpu.VMEM((4, ch, 2 * tok), F32),
            pltpu.VMEM((2, 2, ch, 2 * tok), F32),
            pltpu.VMEM((2, ch, 2 * tok), F32),
            dma((planes, SLOTS)), dma((planes, SLOTS)), dma((8,)), dma((1,)), dma((3,)),
            dma((n_sends,)), dma((n_sends,)), dma((4,)), dma((1,)), dma((2,)),
        ],
        compiler_params=pltpu.CompilerParams(
            collective_id=0, has_side_effects=True, vmem_limit_bytes=52 * 2**20),
    )(query_rows, key_rows, value_rows, tile_mask, head_weight.T)
    moment = step_index[0].astype(F32)
    sigma_now = flow_sigma(moment)
    step_size = flow_sigma(moment + 1.0) - sigma_now
    return guided, latent - sigma_now * guided, latent + step_size * guided


def solution(mesh):
    rows = P(("groups", "frame"), None)
    return jax.shard_map(
        per_device,
        mesh=mesh,
        in_specs=(rows, rows, rows, rows, P(), rows, P("groups")),
        out_specs=(rows, rows, rows),
        check_vma=False,
    )
```

```python
import functools
import math

import jax
import jax.numpy as jnp
from jax import lax
from jax.experimental import pallas as pl
from jax.experimental.pallas import tpu as pltpu
from jax.sharding import PartitionSpec as P

HEADS = 20
HD = 128
SH = 4
SW = 8
SAMPLE_STEPS = 50
GUIDANCE = 5.0
FLOW_SHIFT = 5.0

NT = (((1,), (1,)), ((), ()))
F32 = jnp.float32
BF16 = jnp.bfloat16

GR = SH // 2 + 1
GC = SW // 2 + 1
SLOTS = GR * GC


def flow_sigma(moment):
    remain = 1.0 - moment / SAMPLE_STEPS
    return FLOW_SHIFT * remain / (1.0 + (FLOW_SHIFT - 1.0) * remain)


def kernel(
    planes, tile_frames, tok, ch,
    q_hbm, k_hbm, v_hbm, mask_hbm, wt_hbm,
    out_ref,
    mask_ref, wt_ref, kwin, vwin, qwin, mwin, vloc, vsrc, wbuf, vel, vsib, vpart,
    k_sem, v_sem, q_sem, m_sem, x_sem,
    ks_send, vs_send, qs_send, m_send, x_send,
):
    half = q_hbm.shape[1] // 2
    pairs = half // (2 * HD)
    f = lax.axis_index("frame")
    c = f % 2
    pcol = f // 2 % 2
    prow = f // 4 % 2
    ft = f // 8 % tile_frames
    branch = f // (8 * tile_frames)
    sibling = f + 1 - 2 * c
    partner = f + 8 * tile_frames * (1 - 2 * branch)
    dvert = 4 - 8 * prow
    dhoriz = 2 - 4 * pcol
    base_even = f - c
    edge_u = 1 - prow
    edge_v = 1 - pcol
    own_base = 2 * (pcol * c + (1 - pcol) * (1 - c))
    sib_base = 2 - own_base
    steps = [0] + ([-1, 1] if planes == 3 else [])

    def plane_of(df):
        return df + 1 if planes == 3 else 0

    def exists(df):
        return jnp.logical_and(ft + df >= 0, ft + df < tile_frames)

    def guard(df, extra=None):
        conds = []
        if df != 0:
            conds.append(exists(df))
        if extra is not None:
            conds.append(extra)
        if not conds:
            return lambda fn: fn()
        return pl.when(functools.reduce(jnp.logical_and, conds))

    v_copy = pltpu.make_async_copy(v_hbm, vloc, x_sem.at[2])
    v_copy.start()
    mask_copy = pltpu.make_async_copy(mask_hbm, mask_ref, x_sem.at[3])
    mask_copy.start()
    wt_copy = pltpu.make_async_copy(wt_hbm, wt_ref, x_sem.at[4])
    wt_copy.start()

    def rel(u, i):
        ur = prow * u + (1 - prow) * (1 - u)
        v = pcol * i + (1 - pcol) * (1 - i)
        return ur, v

    local = []
    for u in range(2):
        for i in range(2):
            ur, v = rel(u, i)
            row = pl.multiple_of((u * 2 + v) * tok, tok)
            wr = own_base + i
            slot = (1 + ur) * GC + 1 + wr
            cols = pl.ds(pl.multiple_of(c * half, half), half)
            pltpu.make_async_copy(
                k_hbm.at[pl.ds(row, tok), cols],
                kwin.at[plane_of(0), slot], k_sem.at[plane_of(0), slot]).start()
            pltpu.make_async_copy(
                q_hbm.at[pl.ds(row, tok), cols],
                qwin.at[wr * 2 + ur], q_sem.at[wr * 2 + ur]).start()

    barrier = pltpu.get_barrier_semaphore()
    block = f - f % 8
    greeted = 0
    for df in steps:
        for other in range(8):
            target = block + 8 * df + other
            if df == 0:
                @pl.when(target != f)
                def _(target=target):
                    pl.semaphore_signal(barrier, inc=1, device_id={"frame": target},
                                        device_id_type=pl.DeviceIdType.MESH)
            else:
                @pl.when(exists(df))
                def _(target=target):
                    pl.semaphore_signal(barrier, inc=1, device_id={"frame": target},
                                        device_id_type=pl.DeviceIdType.MESH)
        if df == 0:
            greeted = 7
        else:
            greeted = greeted + 8 * exists(df).astype(jnp.int32)
    pl.semaphore_signal(barrier, inc=1, device_id={"frame": partner},
                        device_id_type=pl.DeviceIdType.MESH)
    pl.semaphore_wait(barrier, greeted + 1)

    sends = []
    number = 0
    edge_core = c == 1 - pcol
    for df in steps:
        there = plane_of(-df)
        for core in range(2):
            target = base_even + 8 * df + core + dvert
            for i in range(2):
                v = pcol * i + (1 - pcol) * (1 - i)
                sends.append((df, None, target, core, edge_u * 2 + v,
                              0 * GC + 1 + own_base + i, there))
        for core in range(2):
            target = base_even + 8 * df + core + dvert + dhoriz
            sends.append((df, edge_core, target, core, edge_u * 2 + edge_v, 0, there))
        for core in range(2):
            target = base_even + 8 * df + core + dhoriz
            for u in range(2):
                ur = prow * u + (1 - prow) * (1 - u)
                sends.append((df, edge_core, target, core, u * 2 + edge_v,
                              (1 + ur) * GC, there))
        for u in range(2):
            for i in range(2):
                ur, v = rel(u, i)
                slot = (1 + ur) * GC + 1 + own_base + i
                if df == 0:
                    sends.append((df, None, sibling, None, u * 2 + v, slot, there))
                else:
                    for core in range(2):
                        sends.append((df, None, base_even + 8 * df + core, core,
                                      u * 2 + v, slot, there))

    def k_copy(n):
        df, cond, target, core, tile, slot, there = sends[n]
        core = 1 - c if core is None else core
        return pltpu.make_async_remote_copy(
            src_ref=k_hbm.at[pl.ds(pl.multiple_of(tile * tok, tok), tok),
                             pl.ds(pl.multiple_of(core * half, half), half)],
            dst_ref=kwin.at[there, slot],
            send_sem=ks_send.at[n], recv_sem=k_sem.at[there, slot],
            device_id={"frame": target}, device_id_type=pl.DeviceIdType.MESH)

    def v_copy_out(n):
        df, cond, target, core, tile, slot, there = sends[n]
        core = 1 - c if core is None else core
        return pltpu.make_async_remote_copy(
            src_ref=vsrc.at[tile, core],
            dst_ref=vwin.at[there, slot],
            send_sem=vs_send.at[n], recv_sem=v_sem.at[there, slot],
            device_id={"frame": target}, device_id_type=pl.DeviceIdType.MESH)

    def each_send(make, act):
        for n, (df, cond, *_) in enumerate(sends):
            guard(df, cond)(lambda n=n: act(make(n)))

    each_send(k_copy, lambda copy: copy.start())

    def q_copy(u, i):
        ur, v = rel(u, i)
        place = (own_base + i) * 2 + ur
        return pltpu.make_async_remote_copy(
            src_ref=q_hbm.at[pl.ds(pl.multiple_of((u * 2 + v) * tok, tok), tok),
                             pl.ds(pl.multiple_of((1 - c) * half, half), half)],
            dst_ref=qwin.at[place],
            send_sem=qs_send.at[u * 2 + i], recv_sem=q_sem.at[place],
            device_id={"frame": sibling}, device_id_type=pl.DeviceIdType.MESH)

    for u in range(2):
        for i in range(2):
            q_copy(u, i).start()

    mask_copy.wait()
    lane = lax.broadcasted_iota(jnp.int32, (1, 2 * tok), 1)
    for i in range(2):
        v = pcol * i + (1 - pcol) * (1 - i)
        for df in steps:
            for rr in range(GR):
                for dj in range(3):
                    col = pcol * dj + (1 - pcol) * (2 - dj)
                    row0 = prow * rr + (1 - prow) * (2 - rr)
                    first = mask_ref[edge_u * 2 + v, 9 * (df + 1) + 3 * row0 + col]
                    if rr > 0:
                        row1 = prow * (rr - 1) + (1 - prow) * (3 - rr)
                        second = mask_ref[prow * 2 + v, 9 * (df + 1) + 3 * row1 + col]
                    else:
                        second = 0
                    value = jnp.where(lane < tok, first, second)
                    if df != 0:
                        value = value * exists(df).astype(jnp.int32)
                    mwin[own_base + i, pl.ds((plane_of(df) * GR + rr) * 3 + dj, 1), :] = (
                        jnp.where(value > 0, 3e38, -1e30).astype(F32))
    m_copy = pltpu.make_async_remote_copy(
        src_ref=mwin.at[pl.ds(own_base, 2)], dst_ref=mwin.at[pl.ds(own_base, 2)],
        send_sem=m_send.at[0], recv_sem=m_sem.at[0],
        device_id={"frame": sibling}, device_id_type=pl.DeviceIdType.MESH)
    m_copy.start()

    v_copy.wait()
    wt_copy.wait()

    def project(j, _):
        parts = []
        for e in range(2):
            cols = pl.ds(pl.multiple_of((2 * j + e) * HD, HD), HD)
            parts.append(lax.dot_general(wt_ref[:, cols], vloc[:, cols], NT,
                                         preferred_element_type=F32))
        side = j // pairs
        rows = pl.ds(pl.multiple_of((j % pairs) * ch, ch), ch)
        for t in range(4):
            both = jnp.concatenate(
                [part[:, t * tok:(t + 1) * tok] for part in parts], axis=1).astype(BF16)
            vsrc[t, side, rows, :] = both
        return 0

    lax.fori_loop(0, 2 * pairs, project, 0)
    each_send(v_copy_out, lambda copy: copy.start())
    for u in range(2):
        for i in range(2):
            ur, v = rel(u, i)
            slot = (1 + ur) * GC + 1 + own_base + i
            vwin[plane_of(0), slot] = vsrc[u * 2 + v, c]
    for df in steps[1:]:
        @pl.when(jnp.logical_not(exists(df)))
        def _(df=df):
            kwin[plane_of(df)] = jnp.zeros(kwin.shape[1:], kwin.dtype)
            vwin[plane_of(df)] = jnp.zeros(vwin.shape[1:], vwin.dtype)

    for place in range(8):
        pltpu.make_async_copy(qwin.at[place], qwin.at[place], q_sem.at[place]).wait()
    m_back = pltpu.make_async_remote_copy(
        src_ref=mwin.at[pl.ds(sib_base, 2)], dst_ref=mwin.at[pl.ds(sib_base, 2)],
        send_sem=m_send.at[0], recv_sem=m_sem.at[0],
        device_id={"frame": sibling}, device_id_type=pl.DeviceIdType.MESH)
    m_back.wait_recv()
    for df in steps:
        def arrive(df=df):
            p = plane_of(df)
            for slot in range(SLOTS):
                pltpu.make_async_copy(kwin.at[p, slot], kwin.at[p, slot],
                                      k_sem.at[p, slot]).wait()
        guard(df)(arrive)

    scale = math.log2(math.e) / math.sqrt(HD)

    def weigh(hp, _):
        for wr in range(4):
            ncol = min(3, GC - wr)
            for e in range(2):
                cols = pl.ds(pl.multiple_of((2 * hp + e) * HD, HD), HD)
                query = qwin[2 * wr:2 * wr + 2, :, cols].reshape(2 * tok, HD)
                blocks = []
                top = None
                for p in range(planes):
                    for rr in range(GR):
                        first = rr * GC + wr
                        keys = kwin[p, first:first + ncol, :, cols].reshape(ncol * tok, HD)
                        s = lax.dot_general(keys, query, NT, preferred_element_type=F32)
                        for dj in range(ncol):
                            line = (p * GR + rr) * 3 + dj
                            part = jnp.minimum(s[dj * tok:(dj + 1) * tok] * scale,
                                               mwin[wr, line:line + 1, :])
                            blocks.append(part)
                            here = jnp.max(part.reshape(tok // 8, 8, 2 * tok), axis=0)
                            top = here if top is None else jnp.maximum(top, here)
                top = jnp.max(top, axis=0, keepdims=True)
                total = None
                grown = []
                for part in blocks:
                    g = jnp.exp2(part - top)
                    grown.append(g)
                    here = jnp.sum(g.reshape(tok // 8, 8, 2 * tok), axis=0)
                    total = here if total is None else total + here
                inverse = 1.0 / jnp.sum(total, axis=0, keepdims=True)
                for n, g in enumerate(grown):
                    start = n * 2 * tok + e * tok
                    wbuf[hp, wr, start:start + tok, :] = (g * inverse).astype(BF16)
        return 0

    lax.fori_loop(0, pairs, weigh, 0)

    own_half_slots = own_base + 1
    for df in steps:
        def arrive(df=df):
            p = plane_of(df)
            for slot in range(SLOTS):
                copy = pltpu.make_async_copy(vwin.at[p, slot], vwin.at[p, slot], v_sem.at[p, slot])
                rr, cc = slot // GC, slot % GC
                if df == 0 and rr > 0 and cc > 0:
                    side = (cc - 1) // 2
                    pl.when(own_base != 2 * side)(lambda copy=copy: copy.wait())
                else:
                    copy.wait()
        guard(df)(arrive)

    def gather(hp, acc):
        rows = pl.ds(pl.multiple_of(hp * ch, ch), ch)
        result = []
        for wr in range(4):
            ncol = min(3, GC - wr)
            total = acc[wr]
            n = 0
            for p in range(planes):
                for rr in range(GR):
                    for dj in range(ncol):
                        slot = rr * GC + wr + dj
                        total = total + jnp.dot(
                            vwin[p, slot, rows, :],
                            wbuf[hp, wr, n * 2 * tok:(n + 1) * 2 * tok, :],
                            preferred_element_type=F32)
                        n += 1
            result.append(total)
        return tuple(result)

    acc = lax.fori_loop(0, pairs, gather,
                        tuple(jnp.zeros((ch, 2 * tok), F32) for _ in range(4)))
    for wr in range(4):
        vel[wr] = acc[wr]

    s_copy = pltpu.make_async_remote_copy(
        src_ref=vel.at[pl.ds(sib_base, 2)], dst_ref=vsib.at[0],
        send_sem=x_send.at[0], recv_sem=x_sem.at[0],
        device_id={"frame": sibling}, device_id_type=pl.DeviceIdType.MESH)
    s_copy.start()
    s_copy.wait_recv()
    mine = vel[pl.ds(own_base, 2)] + vsib[0]
    vsib[1] = mine
    p_copy = pltpu.make_async_remote_copy(
        src_ref=vsib.at[1], dst_ref=vpart,
        send_sem=x_send.at[1], recv_sem=x_sem.at[1],
        device_id={"frame": partner}, device_id_type=pl.DeviceIdType.MESH)
    p_copy.start()
    p_copy.wait_recv()
    left = lax.broadcasted_iota(jnp.int32, (ch, 2 * tok), 1) < tok
    for place, held in ((branch, vsib.at[1]), (1 - branch, vpart)):
        first, second = held[1 - pcol], held[pcol]
        out_ref[place, :, pl.ds(pl.multiple_of(edge_u * 2 * tok, 2 * tok), 2 * tok)] = (
            jnp.where(left, first, pltpu.roll(second, tok, 1)))
        out_ref[place, :, pl.ds(pl.multiple_of(prow * 2 * tok, 2 * tok), 2 * tok)] = (
            jnp.where(left, pltpu.roll(first, tok, 1), second))

    each_send(k_copy, lambda copy: copy.wait_send())
    each_send(v_copy_out, lambda copy: copy.wait_send())
    for u in range(2):
        for i in range(2):
            q_copy(u, i).wait_send()
    m_copy.wait_send()
    s_copy.wait_send()
    p_copy.wait_send()


def per_device(query_rows, key_rows, value_rows, tile_mask, head_weight, latent, step_index):
    frame_count = lax.axis_size("frame")
    tile_frames = frame_count // (2 * (SH // 2) * (SW // 2))
    planes = 3 if tile_frames > 1 else 1
    rows, width = query_rows.shape
    tok = rows // 4
    ch = head_weight.shape[1]
    half = width // 2
    pairs = half // (2 * HD)
    n_sends = 14 + (planes - 1) * 18
    lines = -(-planes * GR * 3 // 8) * 8
    dma = pltpu.SemaphoreType.DMA
    hbm = pl.BlockSpec(memory_space=pltpu.HBM)
    both = pl.pallas_call(
        functools.partial(kernel, planes, tile_frames, tok, ch),
        out_shape=jax.ShapeDtypeStruct((2, ch, rows), F32),
        in_specs=[hbm] * 5,
        out_specs=pl.BlockSpec(memory_space=pltpu.VMEM),
        scratch_shapes=[
            pltpu.SMEM(tile_mask.shape, jnp.int32),
            pltpu.VMEM((ch, width), BF16),
            pltpu.VMEM((planes, SLOTS, tok, half), BF16),
            pltpu.VMEM((planes, SLOTS, pairs * ch, 2 * tok), BF16),
            pltpu.VMEM((8, tok, half), BF16),
            pltpu.VMEM((4, lines, 2 * tok), F32),
            pltpu.VMEM((rows, width), BF16),
            pltpu.VMEM((4, 2, pairs * ch, 2 * tok), BF16),
            pltpu.VMEM((pairs, 4, planes * GR * 3 * 2 * tok, 2 * tok), BF16),
            pltpu.VMEM((4, ch, 2 * tok), F32),
            pltpu.VMEM((2, 2, ch, 2 * tok), F32),
            pltpu.VMEM((2, ch, 2 * tok), F32),
            dma((planes, SLOTS)), dma((planes, SLOTS)), dma((8,)), dma((1,)), dma((5,)),
            dma((n_sends,)), dma((n_sends,)), dma((4,)), dma((1,)), dma((2,)),
        ],
        compiler_params=pltpu.CompilerParams(
            collective_id=0, has_side_effects=True, vmem_limit_bytes=63 * 2**20),
    )(query_rows, key_rows, value_rows, tile_mask, head_weight.T)
    moment = step_index[0].astype(F32)
    sigma_now = flow_sigma(moment)
    step_size = flow_sigma(moment + 1.0) - sigma_now
    guided = both[1] + GUIDANCE * (both[0] - both[1])
    turned = latent.T
    return guided.T, (turned - sigma_now * guided).T, (turned + step_size * guided).T


def solution(mesh):
    rows = P(("groups", "frame"), None)
    return jax.shard_map(
        per_device,
        mesh=mesh,
        in_specs=(rows, rows, rows, rows, P(), rows, P("groups")),
        out_specs=(rows, rows, rows),
        check_vma=False,
    )
```

```python
import functools
import math

import jax
import jax.numpy as jnp
from jax import lax
from jax.experimental import pallas as pl
from jax.experimental.pallas import tpu as pltpu
from jax.sharding import PartitionSpec as P

HEADS = 20
HD = 128
SH = 4
SW = 8
SAMPLE_STEPS = 50
GUIDANCE = 5.0
FLOW_SHIFT = 5.0

NT = (((1,), (1,)), ((), ()))
F32 = jnp.float32
BF16 = jnp.bfloat16

GR = SH // 2 + 1
GC = SW // 2 + 1
SLOTS = GR * GC


def flow_sigma(moment):
    remain = 1.0 - moment / SAMPLE_STEPS
    return FLOW_SHIFT * remain / (1.0 + (FLOW_SHIFT - 1.0) * remain)


def kernel(
    planes, tile_frames, tok, ch,
    q_hbm, k_hbm, v_hbm, mask_hbm, wt_hbm,
    out_ref,
    mask_ref, wt_ref, kwin, vwin, qwin, mwin, vloc, vsrc, wbuf, vel, vsib, vsum, vpart,
    k_sem, v_sem, q_sem, m_sem, x_sem,
    ks_send, vs_send, qs_send, m_send, x_send, f_send,
):
    half = q_hbm.shape[1] // 2
    pairs = half // (2 * HD)
    f = lax.axis_index("frame")
    c = f % 2
    pcol = f // 2 % 2
    prow = f // 4 % 2
    ft = f // 8 % tile_frames
    branch = f // (8 * tile_frames)
    sibling = f + 1 - 2 * c
    partner = f + 8 * tile_frames * (1 - 2 * branch)
    dvert = 4 - 8 * prow
    dhoriz = 2 - 4 * pcol
    base_even = f - c
    edge_u = 1 - prow
    edge_v = 1 - pcol
    own_base = 2 * (pcol * c + (1 - pcol) * (1 - c))
    sib_base = 2 - own_base
    own_group = own_base // 2
    sib_group = 1 - own_group
    steps = [0] + ([-1, 1] if planes == 3 else [])

    def plane_of(df):
        return df + 1 if planes == 3 else 0

    def exists(df):
        return jnp.logical_and(ft + df >= 0, ft + df < tile_frames)

    def guard(df, extra=None):
        conds = []
        if df != 0:
            conds.append(exists(df))
        if extra is not None:
            conds.append(extra)
        if not conds:
            return lambda fn: fn()
        return pl.when(functools.reduce(jnp.logical_and, conds))

    v_copy = pltpu.make_async_copy(v_hbm, vloc, x_sem.at[2])
    v_copy.start()
    mask_copy = pltpu.make_async_copy(mask_hbm, mask_ref, x_sem.at[3])
    mask_copy.start()
    wt_copy = pltpu.make_async_copy(wt_hbm, wt_ref, x_sem.at[4])
    wt_copy.start()

    def rel(u, i):
        ur = prow * u + (1 - prow) * (1 - u)
        v = pcol * i + (1 - pcol) * (1 - i)
        return ur, v

    local = []
    for u in range(2):
        for i in range(2):
            ur, v = rel(u, i)
            row = pl.multiple_of((u * 2 + v) * tok, tok)
            wr = own_base + i
            slot = (1 + ur) * GC + 1 + wr
            cols = pl.ds(pl.multiple_of(c * half, half), half)
            pltpu.make_async_copy(
                k_hbm.at[pl.ds(row, tok), cols],
                kwin.at[plane_of(0), slot], k_sem.at[plane_of(0), slot]).start()
            pltpu.make_async_copy(
                q_hbm.at[pl.ds(row, tok), cols],
                qwin.at[ur * 4 + wr], q_sem.at[ur * 4 + wr]).start()

    barrier = pltpu.get_barrier_semaphore()
    block = f - f % 8
    greeted = 0
    for df in steps:
        for other in range(8):
            target = block + 8 * df + other
            if df == 0:
                @pl.when(target != f)
                def _(target=target):
                    pl.semaphore_signal(barrier, inc=1, device_id={"frame": target},
                                        device_id_type=pl.DeviceIdType.MESH)
            else:
                @pl.when(exists(df))
                def _(target=target):
                    pl.semaphore_signal(barrier, inc=1, device_id={"frame": target},
                                        device_id_type=pl.DeviceIdType.MESH)
        if df == 0:
            greeted = 7
        else:
            greeted = greeted + 8 * exists(df).astype(jnp.int32)
    pl.semaphore_signal(barrier, inc=1, device_id={"frame": partner},
                        device_id_type=pl.DeviceIdType.MESH)
    pl.semaphore_wait(barrier, greeted + 1)

    sends = []
    number = 0
    edge_core = c == 1 - pcol
    for df in steps:
        there = plane_of(-df)
        for i in range(2):
            v = pcol * i + (1 - pcol) * (1 - i)
            for core in range(2):
                target = base_even + 8 * df + core + dvert
                sends.append((df, None, target, core, edge_u * 2 + v,
                              1 + own_base + i, there))
        for core in range(2):
            target = base_even + 8 * df + core + dhoriz
            for u in range(2):
                ur = prow * u + (1 - prow) * (1 - u)
                sends.append((df, edge_core, target, core, u * 2 + edge_v,
                              (1 + ur) * GC, there))
        for u in range(2):
            for i in range(2):
                ur, v = rel(u, i)
                slot = (1 + ur) * GC + 1 + own_base + i
                if df == 0:
                    sends.append((df, None, sibling, None, u * 2 + v, slot, there))
                else:
                    for core in range(2):
                        sends.append((df, None, base_even + 8 * df + core, core,
                                      u * 2 + v, slot, there))

    def k_copy(n):
        df, cond, target, core, tile, slot, there = sends[n]
        core = 1 - c if core is None else core
        return pltpu.make_async_remote_copy(
            src_ref=k_hbm.at[pl.ds(pl.multiple_of(tile * tok, tok), tok),
                             pl.ds(pl.multiple_of(core * half, half), half)],
            dst_ref=kwin.at[there, slot],
            send_sem=ks_send.at[n], recv_sem=k_sem.at[there, slot],
            device_id={"frame": target}, device_id_type=pl.DeviceIdType.MESH)

    def v_copy_out(n):
        df, cond, target, core, tile, slot, there = sends[n]
        core = 1 - c if core is None else core
        return pltpu.make_async_remote_copy(
            src_ref=vsrc.at[tile, core],
            dst_ref=vwin.at[there, slot],
            send_sem=vs_send.at[n], recv_sem=v_sem.at[there, slot],
            device_id={"frame": target}, device_id_type=pl.DeviceIdType.MESH)

    def each_send(make, act):
        for n, (df, cond, *_) in enumerate(sends):
            guard(df, cond)(lambda n=n: act(make(n)))

    each_send(k_copy, lambda copy: copy.start())

    def q_copy(u, i):
        ur, v = rel(u, i)
        place = ur * 4 + own_base + i
        return pltpu.make_async_remote_copy(
            src_ref=q_hbm.at[pl.ds(pl.multiple_of((u * 2 + v) * tok, tok), tok),
                             pl.ds(pl.multiple_of((1 - c) * half, half), half)],
            dst_ref=qwin.at[place],
            send_sem=qs_send.at[u * 2 + i], recv_sem=q_sem.at[place],
            device_id={"frame": sibling}, device_id_type=pl.DeviceIdType.MESH)

    for u in range(2):
        for i in range(2):
            q_copy(u, i).start()

    mask_copy.wait()
    lane = lax.broadcasted_iota(jnp.int32, (1, 2 * tok), 1)
    for df in steps:
        there = 9 * (df + 1)
        for ur in range(2):
            u = edge_u if ur == 0 else prow
            for rr in range(ur, GR):
                di = rr - ur
                row = prow * di + (1 - prow) * (2 - di)
                for k in range(4):
                    sides = []
                    for i in range(2):
                        dj = k - i
                        if 0 <= dj < 3:
                            col = pcol * dj + (1 - pcol) * (2 - dj)
                            v = pcol * i + (1 - pcol) * (1 - i)
                            sides.append(mask_ref[u * 2 + v, there + 3 * row + col])
                        else:
                            sides.append(0)
                    value = jnp.where(lane < tok, sides[0], sides[1])
                    if df != 0:
                        value = value * exists(df).astype(jnp.int32)
                    line = (ur * planes * GR + plane_of(df) * GR + rr) * 4 + k
                    mwin[own_group, line:line + 1, :] = (
                        jnp.where(value > 0, 3e38, -1e30).astype(F32))
    m_copy = pltpu.make_async_remote_copy(
        src_ref=mwin.at[own_group], dst_ref=mwin.at[own_group],
        send_sem=m_send.at[0], recv_sem=m_sem.at[0],
        device_id={"frame": sibling}, device_id_type=pl.DeviceIdType.MESH)
    m_copy.start()

    v_copy.wait()
    wt_copy.wait()

    def project(j, _):
        parts = []
        for e in range(2):
            cols = pl.ds(pl.multiple_of((2 * j + e) * HD, HD), HD)
            parts.append(lax.dot_general(wt_ref[:, cols], vloc[:, cols], NT,
                                         preferred_element_type=F32))
        side = j // pairs
        rows = pl.ds(pl.multiple_of((j % pairs) * ch, ch), ch)
        for t in range(4):
            both = jnp.concatenate(
                [part[:, t * tok:(t + 1) * tok] for part in parts], axis=1).astype(BF16)
            vsrc[t, side, rows, :] = both
        return 0

    lax.fori_loop(0, 2 * pairs, project, 0)
    each_send(v_copy_out, lambda copy: copy.start())
    for u in range(2):
        for i in range(2):
            ur, v = rel(u, i)
            slot = (1 + ur) * GC + 1 + own_base + i
            vwin[plane_of(0), slot] = vsrc[u * 2 + v, c]
    for df in steps[1:]:
        @pl.when(jnp.logical_not(exists(df)))
        def _(df=df):
            kwin[plane_of(df)] = jnp.zeros(kwin.shape[1:], kwin.dtype)
            vwin[plane_of(df)] = jnp.zeros(vwin.shape[1:], vwin.dtype)

    def k_wait(slots):
        for df in steps:
            p = plane_of(df)

            def arrive(p=p):
                for slot in slots:
                    pltpu.make_async_copy(kwin.at[p, slot], kwin.at[p, slot],
                                          k_sem.at[p, slot]).wait()
            guard(df)(arrive)

    def v_wait(slots):
        for df in steps:
            p = plane_of(df)

            def arrive(p=p, df=df):
                for slot in slots:
                    copy = pltpu.make_async_copy(vwin.at[p, slot], vwin.at[p, slot],
                                                 v_sem.at[p, slot])
                    rr, cc = slot // GC, slot % GC
                    if df == 0 and rr > 0 and cc > 0:
                        side = (cc - 1) // 2
                        pl.when(own_group != side)(lambda copy=copy: copy.wait())
                    else:
                        copy.wait()
            guard(df)(arrive)

    def forward(win, sem, kind, df):
        p = plane_of(df)
        return pltpu.make_async_remote_copy(
            src_ref=win.at[p, 1], dst_ref=win.at[p, 0],
            send_sem=f_send.at[p, kind], recv_sem=sem.at[p, 0],
            device_id={"frame": f + dhoriz}, device_id_type=pl.DeviceIdType.MESH)

    def hand_on(win, sem, kind):
        for df in steps:
            guard(df)(lambda df=df: forward(win, sem, kind, df).start())

    inner_slots = list(range(GC, SLOTS))
    outer_slots = list(range(2, GC)) + [0]

    scale = math.log2(math.e) / math.sqrt(HD)

    def weigh(ur, hp):
        for group in range(2):
            ncol = min(4, GC - 2 * group)
            for e in range(2):
                cols = pl.ds(pl.multiple_of((2 * hp + e) * HD, HD), HD)
                place = ur * 4 + 2 * group
                query = qwin[place:place + 2, :, cols].reshape(2 * tok, HD)
                blocks = []
                top = None
                for p in range(planes):
                    for rr in range(ur, GR):
                        first = rr * GC + 2 * group
                        keys = kwin[p, first:first + ncol, :, cols].reshape(ncol * tok, HD)
                        s = lax.dot_general(keys, query, NT, preferred_element_type=F32)
                        for k in range(ncol):
                            line = (ur * planes * GR + p * GR + rr) * 4 + k
                            part = jnp.minimum(s[k * tok:(k + 1) * tok] * scale,
                                               mwin[group, line:line + 1, :])
                            blocks.append(((p * GR + rr) * 4 + k, part))
                            here = jnp.max(part.reshape(tok // 8, 8, 2 * tok), axis=0)
                            top = here if top is None else jnp.maximum(top, here)
                top = jnp.max(top, axis=0, keepdims=True)
                total = None
                grown = []
                for n, part in blocks:
                    g = jnp.exp2(part - top)
                    grown.append((n, g))
                    here = jnp.sum(g.reshape(tok // 8, 8, 2 * tok), axis=0)
                    total = here if total is None else total + here
                inverse = 1.0 / jnp.sum(total, axis=0, keepdims=True)
                for n, g in grown:
                    start = n * 2 * tok + e * tok
                    wbuf[hp, group, start:start + tok, :] = (g * inverse).astype(BF16)

    def gather(rows_of_grid, hp, acc):
        rows = pl.ds(pl.multiple_of(hp * ch, ch), ch)
        result = []
        for group in range(2):
            ncol = min(4, GC - 2 * group)
            total = acc[group]
            for p in range(planes):
                for rr in rows_of_grid:
                    first = rr * GC + 2 * group
                    n = (p * GR + rr) * 4
                    values = jnp.concatenate(
                        [vwin[p, first + k, rows, :] for k in range(ncol)], axis=1)
                    total = total + jnp.dot(
                        values, wbuf[hp, group, n * 2 * tok:(n + ncol) * 2 * tok, :],
                        preferred_element_type=F32)
            result.append(total)
        return tuple(result)

    def weigh_all(ur):
        def body(hp, _):
            weigh(ur, hp)
            return 0
        lax.fori_loop(0, pairs, body, 0)

    def gather_all(rows_of_grid, acc):
        return lax.fori_loop(0, pairs, functools.partial(gather, rows_of_grid), acc)

    nothing = tuple(jnp.zeros((ch, 2 * tok), F32) for _ in range(2))

    def s_copy(ur):
        return pltpu.make_async_remote_copy(
            src_ref=vel.at[ur, sib_group], dst_ref=vsib.at[ur],
            send_sem=x_send.at[ur], recv_sem=x_sem.at[ur],
            device_id={"frame": sibling}, device_id_type=pl.DeviceIdType.MESH)

    def p_copy(ur):
        return pltpu.make_async_remote_copy(
            src_ref=vsum.at[ur], dst_ref=vpart.at[ur],
            send_sem=x_send.at[2 + ur], recv_sem=x_sem.at[5 + ur],
            device_id={"frame": partner}, device_id_type=pl.DeviceIdType.MESH)

    def give(ur, acc):
        for group in range(2):
            vel[ur, group] = acc[group]
        s_copy(ur).start()

    def pass_on(ur):
        s_copy(ur).wait_recv()
        vsum[ur] = vel[ur, own_group] + vsib[ur]
        p_copy(ur).start()

    def finish(ur):
        p_copy(ur).wait_recv()
        u = edge_u if ur == 0 else prow
        lanes = pl.ds(pl.multiple_of(u * 2 * tok, 2 * tok), 2 * tok)
        for place, held in ((branch, vsum), (1 - branch, vpart)):
            value = held[ur]
            out_ref[place, :, lanes] = jnp.where(
                pcol == 1, value, pltpu.roll(value, tok, 1))

    for place in range(8):
        pltpu.make_async_copy(qwin.at[place], qwin.at[place], q_sem.at[place]).wait()
    m_back = pltpu.make_async_remote_copy(
        src_ref=mwin.at[sib_group], dst_ref=mwin.at[sib_group],
        send_sem=m_send.at[0], recv_sem=m_sem.at[0],
        device_id={"frame": sibling}, device_id_type=pl.DeviceIdType.MESH)
    m_back.wait_recv()
    k_wait(inner_slots)
    weigh_all(1)
    k_wait([1])
    hand_on(kwin, k_sem, 0)
    v_wait(inner_slots)
    give(1, gather_all(range(1, GR), nothing))
    pass_on(1)

    k_wait(outer_slots)
    weigh_all(0)
    v_wait([1])
    hand_on(vwin, v_sem, 1)
    acc = gather_all(range(1, GR), nothing)
    finish(1)
    v_wait(outer_slots)
    give(0, gather_all(range(1), acc))
    pass_on(0)
    finish(0)

    each_send(k_copy, lambda copy: copy.wait_send())
    each_send(v_copy_out, lambda copy: copy.wait_send())
    for u in range(2):
        for i in range(2):
            q_copy(u, i).wait_send()
    m_copy.wait_send()
    for ur in range(2):
        s_copy(ur).wait_send()
        p_copy(ur).wait_send()
    for df in steps:
        def sent(df=df):
            forward(kwin, k_sem, 0, df).wait_send()
            forward(vwin, v_sem, 1, df).wait_send()
        guard(df)(sent)


def per_device(query_rows, key_rows, value_rows, tile_mask, head_weight, latent, step_index):
    frame_count = lax.axis_size("frame")
    tile_frames = frame_count // (2 * (SH // 2) * (SW // 2))
    planes = 3 if tile_frames > 1 else 1
    rows, width = query_rows.shape
    tok = rows // 4
    ch = head_weight.shape[1]
    half = width // 2
    pairs = half // (2 * HD)
    n_sends = 12 + (planes - 1) * 16
    lines = -(-2 * planes * GR * 4 // 8) * 8
    dma = pltpu.SemaphoreType.DMA
    hbm = pl.BlockSpec(memory_space=pltpu.HBM)
    both = pl.pallas_call(
        functools.partial(kernel, planes, tile_frames, tok, ch),
        out_shape=jax.ShapeDtypeStruct((2, ch, rows), F32),
        in_specs=[hbm] * 5,
        out_specs=pl.BlockSpec(memory_space=pltpu.VMEM),
        scratch_shapes=[
            pltpu.SMEM(tile_mask.shape, jnp.int32),
            pltpu.VMEM((ch, width), BF16),
            pltpu.VMEM((planes, SLOTS, tok, half), BF16),
            pltpu.VMEM((planes, SLOTS, pairs * ch, 2 * tok), BF16),
            pltpu.VMEM((8, tok, half), BF16),
            pltpu.VMEM((2, lines, 2 * tok), F32),
            pltpu.VMEM((rows, width), BF16),
            pltpu.VMEM((4, 2, pairs * ch, 2 * tok), BF16),
            pltpu.VMEM((pairs, 2, planes * GR * 4 * 2 * tok, 2 * tok), BF16),
            pltpu.VMEM((2, 2, ch, 2 * tok), F32),
            pltpu.VMEM((2, ch, 2 * tok), F32),
            pltpu.VMEM((2, ch, 2 * tok), F32),
            pltpu.VMEM((2, ch, 2 * tok), F32),
            dma((planes, SLOTS)), dma((planes, SLOTS)), dma((8,)), dma((1,)), dma((7,)),
            dma((n_sends,)), dma((n_sends,)), dma((4,)), dma((1,)), dma((4,)), dma((planes, 2)),
        ],
        compiler_params=pltpu.CompilerParams(
            collective_id=0, has_side_effects=True, vmem_limit_bytes=63 * 2**20),
    )(query_rows, key_rows, value_rows, tile_mask, head_weight.T)
    moment = step_index[0].astype(F32)
    sigma_now = flow_sigma(moment)
    step_size = flow_sigma(moment + 1.0) - sigma_now
    guided = both[1] + GUIDANCE * (both[0] - both[1])
    turned = latent.T
    return guided.T, (turned - sigma_now * guided).T, (turned + step_size * guided).T


def solution(mesh):
    rows = P(("groups", "frame"), None)
    return jax.shard_map(
        per_device,
        mesh=mesh,
        in_specs=(rows, rows, rows, rows, P(), rows, P("groups")),
        out_specs=(rows, rows, rows),
        check_vma=False,
    )
```
